512 devices in a mesh: scan: 128 (over z, x, core), bin: 4 (over y).
Axes of the slice: x: 4, y: 4, z: 16, core: 2. Of those that a mesh axis runs over, the one named last changes fastest.
Arguments:
- tile_blocks: bfloat16 [1024, 16, 256, 256], P('scan', 'bin'), may hold values from -0.25 to 0.25
- tile_pattern: int32 [2, 1024], P(None, 'scan'), may hold values from 0 to 255, as said below
- tile_count: int32 [128], P('scan'), may hold values from 1 to 8, as said below
- initial_map: float32 [16, 4, 65536], P('bin', None, 'scan')
- measured: float32 [16, 4, 16384], P('bin', None, 'scan')
- step_size: float32 [1], replicated, may hold values from 0.06 to 0.1
- penalty: float32 [65536], P('scan'), may hold values from 40 to 200
Outputs:
- source_map: float32 [16, 4, 65536], P('bin', None, 'scan')
The draws below stay inside these ranges and needn't reach their ends.
Inputs may be any that keep to these rules, and one draw needn't show every extreme that they name: `tile_pattern`: row 0 names a sensor block of 64; row 1 of slot s names one of the 2 scan tiles (s // 8) * 2 to (s // 8) * 2 + 1. Only the first tile_count[d] slots of index d of scan are live; in every draw some indices have all 8 slots live.
All inputs are finite; a program needn't handle non-finite values.
Results may differ from the reference program's by a relative error of at most 0.00074.
Values may be sent and summed in bfloat16 or wider, within the bound.
A program may use at most 64 MiB of HBM per device.

```python
import math
import jax
import jax.numpy as jnp
from jax import lax

BINS = 16
SNAP = 4
SENSORS = 16384
TILE = 256
TILE_DEV = 2
ITERS = 2
CAP = 8
GROUPS = 128
SLOTS = 1024
POINTS = 65536


def bin_scales(lowest, ratio):
    levels = jnp.arange(BINS, dtype=jnp.float32) / (BINS - 1)
    return lowest * ratio ** levels


def draw_tile_pattern(key, part):
    key_cols, key_rows, key_pick = jax.random.split(jax.random.fold_in(key, 3), 3)
    slot_ids = jnp.arange(SLOTS, dtype=jnp.int32)
    owners = slot_ids // CAP
    offsets = jax.random.randint(key_cols, (GROUPS,), 0, TILE_DEV, dtype=jnp.int32)[owners]
    columns = owners * TILE_DEV + (slot_ids + offsets) % TILE_DEV
    blocks_all = SENSORS // TILE
    sensor_rows = jax.random.randint(key_rows, (SLOTS,), 0, blocks_all, dtype=jnp.int32)
    chosen = jax.random.randint(key_pick, (), 0, SLOTS, dtype=jnp.int32)
    sensor_rows = jnp.where(slot_ids == chosen, blocks_all - 1, sensor_rows)
    return jnp.stack([sensor_rows, columns]).astype(jnp.int32)


def draw_tile_count(key, part):
    key_light, key_heavy, key_pick = jax.random.split(jax.random.fold_in(key, 5), 3)
    light = jax.random.randint(key_light, (GROUPS,), 1, 4, dtype=jnp.int32)
    heavy = jax.random.randint(key_heavy, (GROUPS,), 0, 4, dtype=jnp.int32) == 0
    chosen = jax.random.randint(key_pick, (), 0, GROUPS, dtype=jnp.int32)
    heavy = jnp.logical_or(heavy, jnp.arange(GROUPS, dtype=jnp.int32) == chosen)
    return jnp.where(heavy, CAP, light).astype(jnp.int32)


def draw_initial_map(key, part):
    key_base, key_snap = jax.random.split(jax.random.fold_in(key, 7))
    base = jax.random.truncated_normal(key_base, -3.0, 3.0, (BINS, SNAP, POINTS), jnp.float32)
    snapshot = jax.random.uniform(key_snap, (1, SNAP, 1), jnp.float32, 0.5, 2.0)
    return (base * snapshot * bin_scales(0.316, 10.0)[:, None, None]).astype(jnp.float32)


def draw_measured(key, part):
    key_base = jax.random.fold_in(jax.random.fold_in(key, 9), 0)
    base = jax.random.truncated_normal(key_base, -3.0, 3.0, (BINS, SNAP, SENSORS), jnp.float32)
    return (base * bin_scales(0.6, 3.0)[:, None, None]).astype(jnp.float32)


def steps_of(rng, extent, cuts, smallest, top_value):
    def one(position, parts):
        draws = jax.random.uniform(jax.random.fold_in(jax.random.fold_in(rng, 6), position), (parts,), jnp.float32, smallest / len(cuts), top_value / len(cuts))
        return jnp.repeat(jnp.exp(draws), extent[position] // parts).reshape((-1,) + (1,) * (len(extent) - position - 1))

    level = one(*cuts[0])
    for cut in cuts[1:]:
        level = level * one(*cut)
    return level


def noise(own_key, extent, spread, most, cuts=(), held_as=jnp.bfloat16):
    loudness = steps_of(own_key, extent, cuts, -0.22, 0.18) if cuts else 1.0
    entries = jax.random.normal(own_key, extent, jnp.float32) * spread * loudness
    return jnp.minimum(jnp.maximum(entries, -most), most).astype(held_as)


def setup_inputs(seed: int = 0) -> dict:
    arg_keys = jax.random.split(jax.random.key(seed), 8)
    return {
        "tile_blocks": noise(arg_keys[0], (SLOTS, BINS, TILE, TILE), (2 * TILE) ** -0.5, 0.25, ((0, 128), (1, 4))),
        "tile_pattern": draw_tile_pattern(jax.random.fold_in(arg_keys[7], 71), 0),
        "tile_count": draw_tile_count(jax.random.fold_in(arg_keys[7], 71), 0),
        "initial_map": draw_initial_map(jax.random.fold_in(arg_keys[7], 71), 0),
        "measured": draw_measured(jax.random.fold_in(arg_keys[7], 71), 0),
        "step_size": jnp.clip(jax.random.uniform(arg_keys[5], (1,), jnp.float32, 0.06, 0.1), 0.06, 0.1),
        "penalty": jnp.clip(jnp.exp(math.log(200.0) - 1.609438 * jax.random.uniform(arg_keys[6], (POINTS,), jnp.float32) ** steps_of(arg_keys[6], (POINTS,), ((0, 128),), -0.2, 0.2)), 40.0, 200.0),
    }


def reference(tile_blocks, tile_pattern, tile_count, initial_map, measured, step_size, penalty):
    slot_ids = jnp.arange(SLOTS, dtype=jnp.int32)
    live_mask = (slot_ids % CAP < tile_count[slot_ids // CAP]).astype(jnp.float32)
    block_rows = tile_pattern[0].astype(jnp.int32)
    block_cols = tile_pattern[1].astype(jnp.int32)
    current = initial_map
    for iteration in range(ITERS):
        rounded_map = current.astype(jnp.bfloat16).astype(jnp.float32)

        def forward(running, slot_id):
            matrix = tile_blocks[slot_id].astype(jnp.float32)
            source = lax.dynamic_slice_in_dim(rounded_map, block_cols[slot_id] * TILE, TILE, 2)
            contrib = jnp.einsum('fij,fsj->fsi', matrix, source) * live_mask[slot_id]
            start = block_rows[slot_id] * TILE
            present = lax.dynamic_slice_in_dim(running, start, TILE, 2)
            return (lax.dynamic_update_slice_in_dim(running, present + contrib, start, 2), None)
        predicted = lax.scan(forward, jnp.zeros((BINS, SNAP, SENSORS), jnp.float32), slot_ids)[0]
        residual = predicted - measured
        rounded_residual = residual.astype(jnp.bfloat16).astype(jnp.float32)

        def backward(running, slot_id):
            matrix = tile_blocks[slot_id].astype(jnp.float32)
            source = lax.dynamic_slice_in_dim(rounded_residual, block_rows[slot_id] * TILE, TILE, 2)
            contrib = jnp.einsum('fij,fsi->fsj', matrix, source) * live_mask[slot_id]
            start = block_cols[slot_id] * TILE
            present = lax.dynamic_slice_in_dim(running, start, TILE, 2)
            return (lax.dynamic_update_slice_in_dim(running, present + contrib, start, 2), None)
        gradient = lax.scan(backward, jnp.zeros((BINS, SNAP, POINTS), jnp.float32), slot_ids)[0]
        moved = current - step_size[0] * gradient
        energy = lax.optimization_barrier(jnp.sum(moved * moved, axis=(0, 1)))
        current = moved * jnp.maximum(0.0, 1.0 - step_size[0] * penalty / jnp.sqrt(energy + 1e-06))
    return current
```

```python
import functools

import jax
import jax.numpy as jnp
from jax import lax
from jax.experimental import pallas as pl
from jax.experimental.pallas import tpu as pltpu
from jax.sharding import PartitionSpec as P

ITERS = 2
CORES = 2
ALONG_X = 4
MESH = pl.DeviceIdType.MESH


def kernel(along_z, bins, tiles_hbm, pattern, count, map_ref, measured_ref, step_ref, penalty_ref, out_ref,
           tiles, current, sources, measured, lookup_out, lookup_in, lookup_smem, sums_matrix,
           part_out, part_in, chunk_out, chunk_in, rounded_in, gather_out, gather_in, lhs, energy_out, energy_in,
           tile_sem, smem_sem, send_sem, recv_sem):
    slots, bins_dev, tile, _ = tiles.shape
    group = ALONG_X * CORES
    half = tile // 2
    rows = 16
    snaps = rows // bins_dev
    scan = lax.axis_index("scan")
    y = lax.axis_index("bin")
    core = lax.rem(scan, CORES)
    x = lax.rem(scan // CORES, ALONG_X)
    z = scan // group

    def member(k):
        dx, dc = k // CORES, k % CORES
        there = (z * ALONG_X + lax.rem(x + dx, ALONG_X)) * CORES + (core if dc == 0 else 1 - core)
        return (there, y)

    def along(k):
        return (lax.rem(z + k, along_z) * group + lax.rem(scan, group), y)

    def plane(k):
        return (scan, lax.rem(y + k, bins))

    peers = [member(k) for k in range(1, group)] + [along(k) for k in range(1, along_z)]
    peers += [plane(k) for k in range(1, bins)]
    barrier = pltpu.get_barrier_semaphore()
    for peer in peers:
        pl.semaphore_signal(barrier, inc=1, device_id=peer, device_id_type=MESH)
    loads = []
    for s in range(slots):
        load = pltpu.make_async_copy(tiles_hbm.at[s], tiles.at[s], tile_sem.at[s])
        load.start()
        loads.append(load)

    finish = []

    def exchange(index, src_of, dst, count_, device_of):
        for k in range(1, count_):
            pltpu.make_async_remote_copy(
                src_ref=src_of(k), dst_ref=dst.at[k], send_sem=send_sem.at[index], recv_sem=recv_sem.at[index],
                device_id=device_of(k), device_id_type=MESH,
            ).start()
        whole = dst.at[pl.ds(1, count_ - 1)]
        done = pltpu.make_async_remote_copy(
            src_ref=whole, dst_ref=whole, send_sem=send_sem.at[index], recv_sem=recv_sem.at[index],
            device_id=device_of(1), device_id_type=MESH,
        )
        finish.append(done)
        return done

    lane_slot = lax.broadcasted_iota(jnp.int32, (8, 128), 1) // rows
    names = jnp.zeros((8, 128), jnp.int32)
    live = jnp.zeros((8, 128), jnp.int32)
    for s in range(slots):
        names = jnp.where(lane_slot == s, pattern[0, s], names)
        live = jnp.where(lane_slot == s, (s < count[0]).astype(jnp.int32), live)
    place = lax.rem(z + along_z - names // ALONG_X, along_z)
    for dx in range(ALONG_X):
        there = lax.rem(x + dx, ALONG_X)
        wanted = jnp.where((lax.rem(names, ALONG_X) == there) & (live == 1), place, along_z)
        lookup_out[dx] = wanted
        if dx == 0:
            lookup_in[0] = wanted

    for f in range(bins_dev):
        at = pl.ds(f * snaps, snaps)
        measured[at, :] = measured_ref[f]
        for t in range(2):
            current[t, at, :] = map_ref[f, :, pl.ds(t * tile, tile)]
    row_bin = lax.broadcasted_iota(jnp.int32, (rows, tile), 0) // snaps
    step_size = step_ref[0]
    zeros = jnp.zeros((rows, half), jnp.bfloat16)

    for it in range(ITERS):
        base = 1 + 5 * it
        for t in range(2):
            value = current[t]
            for f in range(bins_dev):
                sources[t, f] = jnp.where(row_bin == f, value, 0.0).astype(jnp.bfloat16)
        own = part_in.at[it]
        out = part_out.at[it]
        for s in range(slots):
            if it == 0:
                loads[s].wait()
            which = lax.rem(pattern[1, s], 2)
            total = jnp.zeros((rows, tile), jnp.float32)
            for f in range(bins_dev):
                total += lax.dot_general(
                    sources[which, f], tiles[s, f], (((1,), (1,)), ((), ())), preferred_element_type=jnp.float32
                )
            low, high = total[:, :half], total[:, half:]
            for dc, value in enumerate((jnp.where(core == 0, low, high), jnp.where(core == 0, high, low))):
                large = value.astype(jnp.bfloat16)
                out[dc, 0, s] = large
                out[dc, 1, s] = (value - large.astype(jnp.float32)).astype(jnp.bfloat16)
        own[0] = out[0]
        if it == 0:
            pl.semaphore_wait(barrier, len(peers))
            told = exchange(0, lambda k: lookup_out.at[k // CORES], lookup_in, group, member)
        parts = exchange(base, lambda k: out.at[k % CORES], own, group, member)
        if it == 0:
            told.wait_recv()
            to_smem = pltpu.make_async_copy(lookup_in, lookup_smem, smem_sem.at[0])
            to_smem.start()
            matrix_row = lax.broadcasted_iota(jnp.int32, (along_z * rows, 128), 0)
            matrix_lane = lax.broadcasted_iota(jnp.int32, (along_z * rows, 128), 1)
            matches = lax.rem(along_z - matrix_row // rows, along_z)
            same = lax.rem(matrix_row, rows) == lax.rem(matrix_lane, rows)
            for k in range(group):
                hit = same & (matches == lookup_in[k, pl.ds(0, 1), :])
                sums_matrix[:, pl.ds(k * 128, 128)] = hit.astype(jnp.float32).astype(jnp.bfloat16)
            to_smem.wait()
        parts.wait_recv()
        chunks = jnp.zeros((along_z * rows, half), jnp.float32)
        for piece in range(2):
            chunks += jnp.dot(
                sums_matrix[...], own[:, piece].reshape(group * slots * rows, half),
                preferred_element_type=jnp.float32,
            )
        chunk_out[it] = chunks.reshape(along_z, rows, half)
        summed = exchange(base + 1, lambda k: chunk_out.at[it, k], chunk_in.at[it], along_z, along)
        total = chunks[:rows] - measured[...]
        summed.wait_recv()
        for k in range(1, along_z):
            total += chunk_in[it, k]
        held = rounded_in.at[it]
        held[0] = total.astype(jnp.bfloat16)
        held[along_z] = zeros
        spread = exchange(base + 2, lambda k: held.at[0], held, along_z, along)
        spread.wait_recv()
        for k in range(group):
            asker = (ALONG_X - k // CORES) % ALONG_X * CORES + k % CORES
            for s in range(slots):
                block = held[lookup_smem[asker, 0, s * rows]]
                if k == 0:
                    gather_in[it, 0, s] = block
                else:
                    gather_out[it, k, s] = block
        gathered = exchange(base + 3, lambda k: gather_out.at[it, k], gather_in.at[it], group, member)
        gathered.wait_recv()
        gradient = jnp.zeros((2 * rows, tile), jnp.float32)
        for s in range(slots):
            which = lax.rem(pattern[1, s], 2)
            mine = gather_in[it, 0, s]
            other = gather_in[it, 1, s]
            for dx in range(1, ALONG_X):
                mine += gather_in[it, dx * CORES, s]
                other += gather_in[it, dx * CORES + 1, s]
            low = jnp.where(core == 0, mine, other).astype(jnp.float32)
            high = jnp.where(core == 0, other, mine).astype(jnp.float32)
            both = jnp.concatenate([low, high], axis=1)
            for f in range(bins_dev):
                one = jnp.where(row_bin == f, both, 0.0)
                for t in range(2):
                    lhs[pl.ds(t * rows, rows), pl.ds(f * tile, tile)] = jnp.where(which == t, one, 0.0).astype(
                        jnp.bfloat16
                    )
            gradient += jnp.dot(
                lhs[...], tiles[s].reshape(bins_dev * tile, tile), preferred_element_type=jnp.float32
            )
        for t in range(2):
            moved = current[t] - step_size * gradient[t * rows:(t + 1) * rows]
            current[t] = moved
            energy_in[it, 0, :, pl.ds(t * tile, tile)] = jnp.sum(moved * moved, axis=0, keepdims=True)
        energy_out[it] = energy_in[it, 0]
        energies = exchange(base + 4, lambda k: energy_out.at[it], energy_in.at[it], bins, plane)
        energies.wait_recv()
        energy = energy_in[it, 0]
        for k in range(1, bins):
            energy += energy_in[it, k]
        factor = jnp.maximum(0.0, 1.0 - step_size * penalty_ref[...] / jnp.sqrt(energy + 1e-06))
        for t in range(2):
            current[t] = current[t] * factor[:, t * tile:(t + 1) * tile]
    for f in range(bins_dev):
        for t in range(2):
            out_ref[f, :, pl.ds(t * tile, tile)] = current[t, pl.ds(f * snaps, snaps), :]
    for done in finish:
        done.wait_send()


def solution(mesh):
    scan, bins = mesh.shape["scan"], mesh.shape["bin"]
    along_z = scan // (ALONG_X * CORES)

    def body(tile_blocks, tile_pattern, tile_count, initial_map, measured, step_size, penalty):
        slots, bins_dev, tile, _ = tile_blocks.shape
        rows, half, group = bins_dev * initial_map.shape[1], tile // 2, ALONG_X * CORES
        points = initial_map.shape[2]
        bf16, f32 = jnp.bfloat16, jnp.float32
        smem = pl.BlockSpec(memory_space=pltpu.SMEM)
        vmem = pl.BlockSpec(memory_space=pltpu.VMEM)
        exchanges = 1 + 5 * ITERS
        return pl.pallas_call(
            functools.partial(kernel, along_z, bins),
            out_shape=jax.ShapeDtypeStruct(initial_map.shape, f32),
            in_specs=[pl.BlockSpec(memory_space=pl.ANY), smem, smem, vmem, vmem, smem, vmem],
            out_specs=vmem,
            scratch_shapes=[
                pltpu.VMEM((slots, bins_dev, tile, tile), bf16),
                pltpu.VMEM((2, rows, tile), f32),
                pltpu.VMEM((2, bins_dev, rows, tile), bf16),
                pltpu.VMEM((rows, half), f32),
                pltpu.VMEM((ALONG_X, 8, 128), jnp.int32),
                pltpu.VMEM((group, 8, 128), jnp.int32),
                pltpu.SMEM((group, 8, 128), jnp.int32),
                pltpu.VMEM((along_z * rows, group * slots * rows), bf16),
                pltpu.VMEM((ITERS, CORES, 2, slots, rows, half), bf16),
                pltpu.VMEM((ITERS, group, 2, slots, rows, half), bf16),
                pltpu.VMEM((ITERS, along_z, rows, half), f32),
                pltpu.VMEM((ITERS, along_z, rows, half), f32),
                pltpu.VMEM((ITERS, along_z + 1, rows, half), bf16),
                pltpu.VMEM((ITERS, group, slots, rows, half), bf16),
                pltpu.VMEM((ITERS, group, slots, rows, half), bf16),
                pltpu.VMEM((2 * rows, bins_dev * tile), bf16),
                pltpu.VMEM((ITERS, 1, points), f32),
                pltpu.VMEM((ITERS, bins, 1, points), f32),
                pltpu.SemaphoreType.DMA((slots,)),
                pltpu.SemaphoreType.DMA((1,)),
                pltpu.SemaphoreType.DMA((exchanges,)),
                pltpu.SemaphoreType.DMA((exchanges,)),
            ],
            compiler_params=pltpu.CompilerParams(
                collective_id=0, has_side_effects=True, vmem_limit_bytes=32 * 1024 * 1024
            ),
        )(tile_blocks, tile_pattern, tile_count, initial_map, measured, step_size, penalty.reshape(1, points))

    in_specs = (
        P("scan", "bin", None, None),
        P(None, "scan"),
        P("scan"),
        P("bin", None, "scan"),
        P("bin", None, "scan"),
        P(),
        P("scan"),
    )
    return jax.shard_map(body, mesh=mesh, in_specs=in_specs, out_specs=P("bin", None, "scan"), check_vma=False)
```

```python
import functools

import jax
import jax.numpy as jnp
from jax import lax
from jax.experimental import pallas as pl
from jax.experimental.pallas import tpu as pltpu
from jax.sharding import PartitionSpec as P

ITERS = 2
CORES = 2
ALONG_X = 4
MESH = pl.DeviceIdType.MESH


def kernel(along_z, bins, tiles_hbm, pattern_hbm, count, map_hbm, measured_hbm, step_ref, penalty_hbm, out_ref,
           pattern, map_ref, measured_ref, penalty_ref, tiles, current, sources, measured, lookup_out, lookup_in, lookup_smem, sums_matrix,
           part_out, part_in, chunk_out, chunk_in, rounded_in, gather_out, gather_in, lhs, energy_out, energy_in,
           tile_sem, input_sem, smem_sem, send_sem, recv_sem):
    slots, bins_dev, tile, _ = tiles.shape
    group = ALONG_X * CORES
    half = tile // 2
    rows = 16
    snaps = rows // bins_dev
    scan = lax.axis_index("scan")
    y = lax.axis_index("bin")
    core = lax.rem(scan, CORES)
    x = lax.rem(scan // CORES, ALONG_X)
    z = scan // group

    def member(k):
        dx, dc = k // CORES, k % CORES
        there = (z * ALONG_X + lax.rem(x + dx, ALONG_X)) * CORES + (core if dc == 0 else 1 - core)
        return (there, y)

    def along(k):
        return (lax.rem(z + k, along_z) * group + lax.rem(scan, group), y)

    def plane(k):
        return (scan, lax.rem(y + k, bins))

    z_order = sorted(range(1, along_z), key=lambda k: -min(k, along_z - k))
    group_order = sorted(range(1, group), key=lambda k: (-min(k // CORES, ALONG_X - k // CORES), -(k % CORES)))
    plane_order = sorted(range(1, bins), key=lambda k: -min(k, bins - k))
    peers = [along(k) for k in z_order] + [member(k) for k in group_order] + [plane(k) for k in plane_order]
    inputs = []
    for i, (there, here) in enumerate((
        (pattern_hbm, pattern), (map_hbm, map_ref), (measured_hbm, measured_ref), (penalty_hbm, penalty_ref),
    )):
        load = pltpu.make_async_copy(there, here, input_sem.at[i])
        load.start()
        inputs.append(load)
    barrier = pltpu.get_barrier_semaphore()
    for peer in peers:
        pl.semaphore_signal(barrier, inc=1, device_id=peer, device_id_type=MESH)
    loads = []
    for s in range(slots):
        load = pltpu.make_async_copy(tiles_hbm.at[s], tiles.at[s], tile_sem.at[s])
        load.start()
        loads.append(load)

    for load in inputs:
        load.wait()
    finish = []

    def exchange(index, src_of, dst, order, device_of):
        for k in order:
            pltpu.make_async_remote_copy(
                src_ref=src_of(k), dst_ref=dst.at[k], send_sem=send_sem.at[index], recv_sem=recv_sem.at[index],
                device_id=device_of(k), device_id_type=MESH,
            ).start()
        whole = dst.at[pl.ds(1, len(order))]
        done = pltpu.make_async_remote_copy(
            src_ref=whole, dst_ref=whole, send_sem=send_sem.at[index], recv_sem=recv_sem.at[index],
            device_id=device_of(1), device_id_type=MESH,
        )
        finish.append(done)
        return done

    lane_slot = lax.broadcasted_iota(jnp.int32, (8, 128), 1) // rows
    names = jnp.zeros((8, 128), jnp.int32)
    live = jnp.zeros((8, 128), jnp.int32)
    for s in range(slots):
        names = jnp.where(lane_slot == s, pattern[0, s], names)
        live = jnp.where(lane_slot == s, (s < count[0]).astype(jnp.int32), live)
    place = lax.rem(z + along_z - names // ALONG_X, along_z)
    for dx in range(ALONG_X):
        there = lax.rem(x + dx, ALONG_X)
        wanted = jnp.where((lax.rem(names, ALONG_X) == there) & (live == 1), place, along_z)
        lookup_out[dx] = wanted
        if dx == 0:
            lookup_in[0] = wanted

    for f in range(bins_dev):
        at = pl.ds(f * snaps, snaps)
        measured[at, :] = measured_ref[f]
        for t in range(2):
            current[t, at, :] = map_ref[f, :, pl.ds(t * tile, tile)]
    row_bin = lax.broadcasted_iota(jnp.int32, (rows, tile), 0) // snaps
    step_size = step_ref[0]
    zeros = jnp.zeros((rows, half), jnp.bfloat16)

    for it in range(ITERS):
        base = 1 + 5 * it
        for t in range(2):
            value = current[t]
            for f in range(bins_dev):
                sources[t, f] = jnp.where(row_bin == f, value, 0.0).astype(jnp.bfloat16)
        own = part_in.at[it]
        out = part_out.at[it]
        for s in range(slots):
            if it == 0:
                loads[s].wait()
            which = lax.rem(pattern[1, s], 2)
            total = jnp.zeros((rows, tile), jnp.float32)
            for f in range(bins_dev):
                total += lax.dot_general(
                    sources[which, f], tiles[s, f], (((1,), (1,)), ((), ())), preferred_element_type=jnp.float32
                )
            low, high = total[:, :half], total[:, half:]
            for dc, value in enumerate((jnp.where(core == 0, low, high), jnp.where(core == 0, high, low))):
                large = value.astype(jnp.bfloat16)
                out[dc, s, :, pl.ds(0, half)] = large
                out[dc, s, :, pl.ds(half, half)] = (value - large.astype(jnp.float32)).astype(jnp.bfloat16)
        own[0] = out[0]
        if it == 0:
            pl.semaphore_wait(barrier, len(peers))
            told = exchange(0, lambda k: lookup_out.at[k // CORES], lookup_in, group_order, member)
        parts = exchange(base, lambda k: out.at[k % CORES], own, group_order, member)
        if it == 0:
            told.wait_recv()
            to_smem = pltpu.make_async_copy(lookup_in, lookup_smem, smem_sem.at[0])
            to_smem.start()
            matrix_row = lax.broadcasted_iota(jnp.int32, (along_z * rows, 128), 0)
            matrix_lane = lax.broadcasted_iota(jnp.int32, (along_z * rows, 128), 1)
            matches = lax.rem(along_z - matrix_row // rows, along_z)
            same = lax.rem(matrix_row, rows) == lax.rem(matrix_lane, rows)
            for k in range(group):
                hit = same & (matches == lookup_in[k, pl.ds(0, 1), :])
                sums_matrix[:, pl.ds(k * 128, 128)] = hit.astype(jnp.float32).astype(jnp.bfloat16)
            to_smem.wait()
        parts.wait_recv()
        chunks = jnp.dot(
            sums_matrix[...], own[...].reshape(group * slots * rows, tile), preferred_element_type=jnp.float32
        )
        chunks = chunks[:, :half] + chunks[:, half:]
        chunk_out[it] = chunks.reshape(along_z, rows, half)
        summed = exchange(base + 1, lambda k: chunk_out.at[it, k], chunk_in.at[it], z_order, along)
        total = chunks[:rows] - measured[...]
        summed.wait_recv()
        for k in range(1, along_z):
            total += chunk_in[it, k]
        held = rounded_in.at[it]
        held[0] = total.astype(jnp.bfloat16)
        held[along_z] = zeros
        spread = exchange(base + 2, lambda k: held.at[0], held, z_order, along)
        spread.wait_recv()
        for k in range(group):
            asker = (ALONG_X - k // CORES) % ALONG_X * CORES + k % CORES
            for s in range(slots):
                block = held[lookup_smem[asker, 0, s * rows]]
                if k == 0:
                    gather_in[it, 0, s] = block
                else:
                    gather_out[it, k, s] = block
        gathered = exchange(base + 3, lambda k: gather_out.at[it, k], gather_in.at[it], group_order, member)
        gathered.wait_recv()
        gradient = jnp.zeros((2 * rows, tile), jnp.float32)
        for s in range(slots):
            which = lax.rem(pattern[1, s], 2)
            mine = gather_in[it, 0, s]
            other = gather_in[it, 1, s]
            for dx in range(1, ALONG_X):
                mine += gather_in[it, dx * CORES, s]
                other += gather_in[it, dx * CORES + 1, s]
            low = jnp.where(core == 0, mine, other).astype(jnp.float32)
            high = jnp.where(core == 0, other, mine).astype(jnp.float32)
            both = jnp.concatenate([low, high], axis=1)
            for f in range(bins_dev):
                one = jnp.where(row_bin == f, both, 0.0)
                for t in range(2):
                    lhs[pl.ds(t * rows, rows), pl.ds(f * tile, tile)] = jnp.where(which == t, one, 0.0).astype(
                        jnp.bfloat16
                    )
            gradient += jnp.dot(
                lhs[...], tiles[s].reshape(bins_dev * tile, tile), preferred_element_type=jnp.float32
            )
        for t in range(2):
            moved = current[t] - step_size * gradient[t * rows:(t + 1) * rows]
            current[t] = moved
            energy_in[it, 0, :, pl.ds(t * tile, tile)] = jnp.sum(moved * moved, axis=0, keepdims=True)
        energy_out[it] = energy_in[it, 0]
        energies = exchange(base + 4, lambda k: energy_out.at[it], energy_in.at[it], plane_order, plane)
        energies.wait_recv()
        energy = energy_in[it, 0]
        for k in range(1, bins):
            energy += energy_in[it, k]
        factor = jnp.maximum(0.0, 1.0 - step_size * penalty_ref[...] / jnp.sqrt(energy + 1e-06))
        for t in range(2):
            current[t] = current[t] * factor[:, t * tile:(t + 1) * tile]
    for f in range(bins_dev):
        for t in range(2):
            out_ref[f, :, pl.ds(t * tile, tile)] = current[t, pl.ds(f * snaps, snaps), :]
    for done in finish:
        done.wait_send()


def solution(mesh):
    scan, bins = mesh.shape["scan"], mesh.shape["bin"]
    along_z = scan // (ALONG_X * CORES)

    def body(tile_blocks, tile_pattern, tile_count, initial_map, measured, step_size, penalty):
        slots, bins_dev, tile, _ = tile_blocks.shape
        rows, half, group = bins_dev * initial_map.shape[1], tile // 2, ALONG_X * CORES
        points = initial_map.shape[2]
        bf16, f32 = jnp.bfloat16, jnp.float32
        exchanges = 1 + 5 * ITERS
        hbm, smem = pl.BlockSpec(memory_space=pltpu.HBM), pl.BlockSpec(memory_space=pltpu.SMEM)
        return pl.pallas_call(
            functools.partial(kernel, along_z, bins),
            out_shape=jax.ShapeDtypeStruct(initial_map.shape, f32),
            in_specs=[hbm, hbm, smem, hbm, hbm, smem, hbm],
            out_specs=pl.BlockSpec(memory_space=pltpu.VMEM),
            scratch_shapes=[
                pltpu.SMEM(tile_pattern.shape, jnp.int32),
                pltpu.VMEM(initial_map.shape, f32),
                pltpu.VMEM(measured.shape, f32),
                pltpu.VMEM((1, points), f32),
                pltpu.VMEM((slots, bins_dev, tile, tile), bf16),
                pltpu.VMEM((2, rows, tile), f32),
                pltpu.VMEM((2, bins_dev, rows, tile), bf16),
                pltpu.VMEM((rows, half), f32),
                pltpu.VMEM((ALONG_X, 8, 128), jnp.int32),
                pltpu.VMEM((group, 8, 128), jnp.int32),
                pltpu.SMEM((group, 8, 128), jnp.int32),
                pltpu.VMEM((along_z * rows, group * slots * rows), bf16),
                pltpu.VMEM((ITERS, CORES, slots, rows, tile), bf16),
                pltpu.VMEM((ITERS, group, slots, rows, tile), bf16),
                pltpu.VMEM((ITERS, along_z, rows, half), f32),
                pltpu.VMEM((ITERS, along_z, rows, half), f32),
                pltpu.VMEM((ITERS, along_z + 1, rows, half), bf16),
                pltpu.VMEM((ITERS, group, slots, rows, half), bf16),
                pltpu.VMEM((ITERS, group, slots, rows, half), bf16),
                pltpu.VMEM((2 * rows, bins_dev * tile), bf16),
                pltpu.VMEM((ITERS, 1, points), f32),
                pltpu.VMEM((ITERS, bins, 1, points), f32),
                pltpu.SemaphoreType.DMA((slots,)),
                pltpu.SemaphoreType.DMA((4,)),
                pltpu.SemaphoreType.DMA((1,)),
                pltpu.SemaphoreType.DMA((exchanges,)),
                pltpu.SemaphoreType.DMA((exchanges,)),
            ],
            compiler_params=pltpu.CompilerParams(
                collective_id=0, has_side_effects=True, vmem_limit_bytes=56 * 1024 * 1024
            ),
        )(tile_blocks, tile_pattern, tile_count, initial_map, measured, step_size, penalty.reshape(1, points))

    in_specs = (
        P("scan", "bin", None, None),
        P(None, "scan"),
        P("scan"),
        P("bin", None, "scan"),
        P("bin", None, "scan"),
        P(),
        P("scan"),
    )
    return jax.shard_map(body, mesh=mesh, in_specs=in_specs, out_specs=P("bin", None, "scan"), check_vma=False)
```

```python
import functools

import jax
import jax.numpy as jnp
from jax import lax
from jax.experimental import pallas as pl
from jax.experimental.pallas import tpu as pltpu
from jax.sharding import PartitionSpec as P

ITERS = 2
CORES = 2
ALONG_X = 4
MESH = pl.DeviceIdType.MESH
LEVELS = 8000.0
BATCHES = 1


def kernel(along_z, bins, tiles_hbm, pattern_hbm, count, map_hbm, measured_hbm, step_ref, penalty_hbm, out_ref,
           pattern, map_ref, measured_ref, penalty_ref, tiles, turned, current, sources, measured, lookup_out, lookup_in, lookup_smem, sums_matrix,
           part_out, part_in, pieces, chunk_out, chunk_in, rounded_in, gather_out, gather_in, energy_out, energy_in,
           tile_sem, input_sem, smem_sem, send_sem, recv_sem):
    slots, bins_dev, tile, _ = tiles.shape
    group = ALONG_X * CORES
    half = tile // 2
    rows = 16
    snaps = rows // bins_dev
    few = slots // BATCHES
    scan = lax.axis_index("scan")
    y = lax.axis_index("bin")
    core = lax.rem(scan, CORES)
    x = lax.rem(scan // CORES, ALONG_X)
    z = scan // group

    def member(k):
        dx, dc = k // CORES, k % CORES
        there = (z * ALONG_X + lax.rem(x + dx, ALONG_X)) * CORES + (core if dc == 0 else 1 - core)
        return (there, y)

    def along(k):
        return (lax.rem(z + k, along_z) * group + lax.rem(scan, group), y)

    def plane(k):
        return (scan, lax.rem(y + k, bins))

    z_order = sorted(range(1, along_z), key=lambda k: -min(k, along_z - k))
    group_order = sorted(range(1, group), key=lambda k: (-min(k // CORES, ALONG_X - k // CORES), -(k % CORES)))
    plane_order = sorted(range(1, bins), key=lambda k: -min(k, bins - k))
    along_at = {k: along(k) for k in z_order}
    member_at = {k: member(k) for k in group_order}
    plane_at = {k: plane(k) for k in plane_order}
    peers = list(along_at.values()) + list(member_at.values()) + list(plane_at.values())
    barrier = pltpu.get_barrier_semaphore()
    for peer in peers:
        pl.semaphore_signal(barrier, inc=1, device_id=peer, device_id_type=MESH)
    inputs = []
    for i, (there, here) in enumerate((
        (pattern_hbm, pattern), (map_hbm, map_ref), (measured_hbm, measured_ref), (penalty_hbm, penalty_ref),
    )):
        load = pltpu.make_async_copy(there, here, input_sem.at[i])
        load.start()
        inputs.append(load)
    loads = []
    for s in range(slots):
        load = pltpu.make_async_copy(tiles_hbm.at[s], tiles.at[s], tile_sem.at[s])
        load.start()
        loads.append(load)

    for load in inputs:
        load.wait()
    finish = []

    sems = iter(range(send_sem.shape[0]))

    def exchange(parts, src_of, dst, devices):
        arrivals = []
        for part in parts:
            sem = next(sems)
            for k in part:
                pltpu.make_async_remote_copy(
                    src_ref=src_of(k), dst_ref=dst.at[k], send_sem=send_sem.at[sem], recv_sem=recv_sem.at[sem],
                    device_id=devices[k], device_id_type=MESH,
                ).start()
            whole = dst.at[pl.ds(min(part), len(part))]
            arrivals.append(pltpu.make_async_remote_copy(
                src_ref=whole, dst_ref=whole, send_sem=send_sem.at[sem], recv_sem=recv_sem.at[sem],
                device_id=devices[part[0]], device_id_type=MESH,
            ))
        finish.extend(arrivals)
        return arrivals

    lane_slot = lax.broadcasted_iota(jnp.int32, (8, 128), 1) // rows
    names = jnp.zeros((8, 128), jnp.int32)
    live = jnp.zeros((8, 128), jnp.int32)
    for s in range(slots):
        names = jnp.where(lane_slot == s, pattern[0, s], names)
        live = jnp.where(lane_slot == s, (s < count[0]).astype(jnp.int32), live)
    place = lax.rem(z + along_z - names // ALONG_X, along_z)
    for dx in range(ALONG_X):
        there = lax.rem(x + dx, ALONG_X)
        wanted = jnp.where((lax.rem(names, ALONG_X) == there) & (live == 1), place, along_z)
        lookup_out[dx] = wanted
        if dx == 0:
            lookup_in[0] = wanted

    for f in range(bins_dev):
        at = pl.ds(f * snaps, snaps)
        measured[at, :] = measured_ref[f]
        for t in range(2):
            current[t, at, :] = map_ref[f, :, pl.ds(t * tile, tile)]
    row_bin = lax.broadcasted_iota(jnp.int32, (rows, tile), 0) // snaps
    step_size = step_ref[0]
    zeros = jnp.zeros((rows, half), jnp.bfloat16)
    lane = lax.broadcasted_iota(jnp.int32, (rows, 128), 1)

    def split(k, s, value):
        at = pl.ds((k * slots + s) * rows, rows)
        large = value.astype(jnp.bfloat16)
        pieces[at, pl.ds(0, half)] = large
        pieces[at, pl.ds(half, half)] = (value - large.astype(jnp.float32)).astype(jnp.bfloat16)


    for it in range(ITERS):
        for t in range(2):
            value = current[t]
            for f in range(bins_dev):
                sources[t, f] = jnp.where(row_bin == f, value, 0.0).astype(jnp.bfloat16)
        own, out = part_in.at[it], part_out.at[it]
        outer = [[k, k + 1] for k in range(CORES, group, CORES)]
        outer = sorted(outer, key=lambda part: group_order.index(part[1])) + [[1]]
        arrivals = []
        for batch in range(BATCHES):
            powers = jnp.zeros((rows, 128), jnp.float32)
            for i in range(few):
                s = batch * few + i
                if it == 0:
                    loads[s].wait()
                which = lax.rem(pattern[1, s], 2)
                total = jnp.zeros((rows, tile), jnp.float32)
                for f in range(bins_dev if it == 0 else 0):
                    total += lax.dot_general(
                        sources[which, f], tiles[s, f], (((1,), (1,)), ((), ())), preferred_element_type=jnp.float32
                    )
                if it > 0:
                    wide = jnp.concatenate([sources[which, f] for f in range(bins_dev)], axis=1)
                    total = jnp.dot(wide, turned[s], preferred_element_type=jnp.float32)
                largest = jnp.max(jnp.abs(total), axis=1, keepdims=True)
                power = jnp.clip(jnp.ceil(jnp.log2(jnp.maximum(largest, 1e-30))), -100.0, 126.0)
                powers = jnp.where(lane == i, power, powers)
                low, high = total[:, :half], total[:, half:]
                mine, other = jnp.where(core == 0, low, high), jnp.where(core == 0, high, low)
                split(0, s, mine)
                for dc, value in enumerate((mine, other)):
                    out[batch, dc, i] = jnp.round(value * (jnp.exp2(-power) * LEVELS)).astype(jnp.int32).astype(jnp.int16)
            for dc in range(CORES):
                out[batch, dc, few] = powers.astype(jnp.int32).astype(jnp.int16)
            if it == 0 and batch < BATCHES - 1:
                continue
            if it == 0:
                pl.semaphore_wait(barrier, len(peers))
                (told,) = exchange([group_order], lambda k: lookup_out.at[k // CORES], lookup_in, member_at)
            for sent in (range(BATCHES) if it == 0 else [batch]):
                arrivals.append(exchange(outer, lambda k: out.at[sent, k % CORES], own.at[sent], member_at))
        if it == 0:
            told.wait_recv()
            to_smem = pltpu.make_async_copy(lookup_in, lookup_smem, smem_sem.at[0])
            to_smem.start()
            matrix_row = lax.broadcasted_iota(jnp.int32, (along_z * rows, 128), 0)
            matrix_lane = lax.broadcasted_iota(jnp.int32, (along_z * rows, 128), 1)
            matches = lax.rem(along_z - matrix_row // rows, along_z)
            same = lax.rem(matrix_row, rows) == lax.rem(matrix_lane, rows)
            for k in range(group):
                hit = same & (matches == lookup_in[k, pl.ds(0, 1), :])
                sums_matrix[:, pl.ds(k * 128, 128)] = hit.astype(jnp.float32).astype(jnp.bfloat16)
        chunks = jnp.zeros((along_z * rows, tile), jnp.float32)
        for batch in range(BATCHES):
            for part, arrival in reversed(list(zip(outer, arrivals[batch]))):
                arrival.wait_recv()
                for k in part:
                    scale = jnp.exp2(own[batch, k, few].astype(jnp.int32).astype(jnp.float32)) * (1.0 / LEVELS)
                    for i in range(few):
                        value = own[batch, k, i].astype(jnp.int32).astype(jnp.float32)
                        split(k, batch * few + i, value * scale[:, i:i + 1])
                if batch == BATCHES - 1:
                    first, width = min(part) // CORES * CORES * slots * rows, CORES * slots * rows
                    chunks += jnp.dot(
                        sums_matrix[:, pl.ds(first, width)], pieces[pl.ds(first, width), :],
                        preferred_element_type=jnp.float32,
                    )
        chunks = chunks[:, :half] + chunks[:, half:]
        chunk_out[it] = chunks.reshape(along_z, rows, half)
        (summed,) = exchange([z_order], lambda k: chunk_out.at[it, k], chunk_in.at[it], along_at)
        total = chunks[:rows] - measured[...]
        if it == 0:
            for s in range(slots):
                for f in range(bins_dev):
                    turned[s, pl.ds(f * tile, tile), :] = tiles[s, f].T
        summed.wait_recv()
        for k in range(1, along_z):
            total += chunk_in[it, k]
        held = rounded_in.at[it]
        held[0] = total.astype(jnp.bfloat16)
        held[along_z] = zeros
        (spread,) = exchange([z_order], lambda k: held.at[0], held, along_at)
        spread.wait_recv()
        if it == 0:
            to_smem.wait()
        arrivals = []
        for batch in range(BATCHES):

            def gather(k):
                asker = (ALONG_X - k // CORES) % ALONG_X * CORES + k % CORES
                there = (gather_out if k else gather_in).at[it, batch, k]
                for i in range(few):
                    there[i] = held[lookup_smem[asker, 0, (batch * few + i) * rows]]
                return there

            arrivals += exchange([group_order], gather, gather_in.at[it, batch], member_at)
            gather(0)
        gradient = [jnp.zeros((rows, tile), jnp.float32) for t in range(2)]
        for s in range(slots):
            batch, i = s // few, s % few
            if i == 0:
                arrivals[batch].wait_recv()
            which = lax.rem(pattern[1, s], 2)
            mine = gather_in[it, batch, 0, i]
            other = gather_in[it, batch, 1, i]
            for dx in range(1, ALONG_X):
                mine += gather_in[it, batch, dx * CORES, i]
                other += gather_in[it, batch, dx * CORES + 1, i]
            low = jnp.where(core == 0, mine, other).astype(jnp.float32)
            high = jnp.where(core == 0, other, mine).astype(jnp.float32)
            both = jnp.concatenate([low, high], axis=1)
            wide = jnp.concatenate([jnp.where(row_bin == f, both, 0.0) for f in range(bins_dev)], axis=1)
            product = jnp.dot(
                wide.astype(jnp.bfloat16), tiles[s].reshape(bins_dev * tile, tile), preferred_element_type=jnp.float32
            )
            for t in range(2):
                gradient[t] += jnp.where(which == t, product, 0.0)
        for t in range(2):
            moved = current[t] - step_size * gradient[t]
            current[t] = moved
            energy_in[it, 0, :, pl.ds(t * tile, tile)] = jnp.sum(moved * moved, axis=0, keepdims=True)
        energy_out[it] = energy_in[it, 0]
        (energies,) = exchange([plane_order], lambda k: energy_out.at[it], energy_in.at[it], plane_at)
        energies.wait_recv()
        energy = energy_in[it, 0]
        for k in range(1, bins):
            energy += energy_in[it, k]
        factor = jnp.maximum(0.0, 1.0 - step_size * penalty_ref[...] / jnp.sqrt(energy + 1e-06))
        for t in range(2):
            current[t] = current[t] * factor[:, t * tile:(t + 1) * tile]
    for f in range(bins_dev):
        for t in range(2):
            out_ref[f, :, pl.ds(t * tile, tile)] = current[t, pl.ds(f * snaps, snaps), :]
    for done in finish:
        done.wait_send()


def solution(mesh):
    scan, bins = mesh.shape["scan"], mesh.shape["bin"]
    along_z = scan // (ALONG_X * CORES)

    def body(tile_blocks, tile_pattern, tile_count, initial_map, measured, step_size, penalty):
        slots, bins_dev, tile, _ = tile_blocks.shape
        rows, half, group = bins_dev * initial_map.shape[1], tile // 2, ALONG_X * CORES
        points, few = initial_map.shape[2], slots // BATCHES
        bf16, f32 = jnp.bfloat16, jnp.float32
        exchanges = 1 + ((ALONG_X + 1) * BATCHES + 3) * ITERS
        hbm, smem = pl.BlockSpec(memory_space=pltpu.HBM), pl.BlockSpec(memory_space=pltpu.SMEM)
        return pl.pallas_call(
            functools.partial(kernel, along_z, bins),
            out_shape=jax.ShapeDtypeStruct(initial_map.shape, f32),
            in_specs=[hbm, hbm, smem, hbm, hbm, smem, hbm],
            out_specs=pl.BlockSpec(memory_space=pltpu.VMEM),
            scratch_shapes=[
                pltpu.SMEM(tile_pattern.shape, jnp.int32),
                pltpu.VMEM(initial_map.shape, f32),
                pltpu.VMEM(measured.shape, f32),
                pltpu.VMEM((1, points), f32),
                pltpu.VMEM((slots, bins_dev, tile, tile), bf16),
                pltpu.VMEM((slots, bins_dev * tile, tile), bf16),
                pltpu.VMEM((2, rows, tile), f32),
                pltpu.VMEM((2, bins_dev, rows, tile), bf16),
                pltpu.VMEM((rows, half), f32),
                pltpu.VMEM((ALONG_X, 8, 128), jnp.int32),
                pltpu.VMEM((group, 8, 128), jnp.int32),
                pltpu.SMEM((group, 8, 128), jnp.int32),
                pltpu.VMEM((along_z * rows, group * slots * rows), bf16),
                pltpu.VMEM((ITERS, BATCHES, CORES, few + 1, rows, half), jnp.int16),
                pltpu.VMEM((ITERS, BATCHES, group, few + 1, rows, half), jnp.int16),
                pltpu.VMEM((group * slots * rows, tile), bf16),
                pltpu.VMEM((ITERS, along_z, rows, half), f32),
                pltpu.VMEM((ITERS, along_z, rows, half), f32),
                pltpu.VMEM((ITERS, along_z + 1, rows, half), bf16),
                pltpu.VMEM((ITERS, BATCHES, group, few, rows, half), bf16),
                pltpu.VMEM((ITERS, BATCHES, group, few, rows, half), bf16),
                pltpu.VMEM((ITERS, 1, points), f32),
                pltpu.VMEM((ITERS, bins, 1, points), f32),
                pltpu.SemaphoreType.DMA((slots,)),
                pltpu.SemaphoreType.DMA((4,)),
                pltpu.SemaphoreType.DMA((1,)),
                pltpu.SemaphoreType.DMA((exchanges,)),
                pltpu.SemaphoreType.DMA((exchanges,)),
            ],
            compiler_params=pltpu.CompilerParams(
                collective_id=0, has_side_effects=True, vmem_limit_bytes=56 * 1024 * 1024
            ),
        )(tile_blocks, tile_pattern, tile_count, initial_map, measured, step_size, penalty.reshape(1, points))

    in_specs = (
        P("scan", "bin", None, None),
        P(None, "scan"),
        P("scan"),
        P("bin", None, "scan"),
        P("bin", None, "scan"),
        P(),
        P("scan"),
    )
    return jax.shard_map(body, mesh=mesh, in_specs=in_specs, out_specs=P("bin", None, "scan"), check_vma=False)
```

```python
import functools

import jax
import jax.numpy as jnp
from jax import lax
from jax.experimental import pallas as pl
from jax.experimental.pallas import tpu as pltpu
from jax.sharding import PartitionSpec as P

ITERS = 2
CORES = 2
ALONG_X = 4
MESH = pl.DeviceIdType.MESH
LEVELS = 14.9
BATCHES = 1


def kernel(along_z, bins, tiles_hbm, pattern_hbm, count, map_hbm, measured_hbm, step_ref, penalty_hbm, out_ref,
           pattern, map_ref, measured_ref, penalty_ref, tiles, turned, current, sources, measured, lookup_out, lookup_in, lookup_smem, sums_matrix,
           part_out, part_in, pieces, chunk_out, chunk_in, rounded_in, gather_out, gather_in, energy_out, energy_in,
           tile_sem, input_sem, smem_sem, send_sem, recv_sem):
    slots, bins_dev, tile, _ = tiles.shape
    group = ALONG_X * CORES
    half = tile // 2
    rows = 16
    snaps = rows // bins_dev
    few = slots // BATCHES
    scan = lax.axis_index("scan")
    y = lax.axis_index("bin")
    core = lax.rem(scan, CORES)
    x = lax.rem(scan // CORES, ALONG_X)
    z = scan // group

    def member(k):
        dx, dc = k // CORES, k % CORES
        there = (z * ALONG_X + lax.rem(x + dx, ALONG_X)) * CORES + (core if dc == 0 else 1 - core)
        return (there, y)

    def along(k):
        return (lax.rem(z + k, along_z) * group + lax.rem(scan, group), y)

    def plane(k):
        return (scan, lax.rem(y + k, bins))

    z_order = sorted(range(1, along_z), key=lambda k: -min(k, along_z - k))
    group_order = sorted(range(1, group), key=lambda k: (-min(k // CORES, ALONG_X - k // CORES), -(k % CORES)))
    plane_order = sorted(range(1, bins), key=lambda k: -min(k, bins - k))
    along_at = {k: along(k) for k in z_order}
    member_at = {k: member(k) for k in group_order}
    plane_at = {k: plane(k) for k in plane_order}
    peers = list(along_at.values()) + list(member_at.values()) + list(plane_at.values())
    barrier = pltpu.get_barrier_semaphore()
    for peer in peers:
        pl.semaphore_signal(barrier, inc=1, device_id=peer, device_id_type=MESH)
    inputs = []
    for i, (there, here) in enumerate((
        (pattern_hbm, pattern), (map_hbm, map_ref), (measured_hbm, measured_ref), (penalty_hbm, penalty_ref),
    )):
        load = pltpu.make_async_copy(there, here, input_sem.at[i])
        load.start()
        inputs.append(load)
    loads = []
    for s in range(slots):
        load = pltpu.make_async_copy(tiles_hbm.at[s], tiles.at[s], tile_sem.at[s])
        load.start()
        loads.append(load)

    for load in inputs:
        load.wait()
    finish = []

    sems = iter(range(send_sem.shape[0]))

    def exchange(parts, src_of, dst, devices):
        arrivals = []
        for part in parts:
            sem = next(sems)
            for k in part:
                pltpu.make_async_remote_copy(
                    src_ref=src_of(k), dst_ref=dst.at[k], send_sem=send_sem.at[sem], recv_sem=recv_sem.at[sem],
                    device_id=devices[k], device_id_type=MESH,
                ).start()
            whole = dst.at[pl.ds(min(part), len(part))]
            arrivals.append(pltpu.make_async_remote_copy(
                src_ref=whole, dst_ref=whole, send_sem=send_sem.at[sem], recv_sem=recv_sem.at[sem],
                device_id=devices[part[0]], device_id_type=MESH,
            ))
        finish.extend(arrivals)
        return arrivals

    lane_slot = lax.broadcasted_iota(jnp.int32, (8, 128), 1) // rows
    names = jnp.zeros((8, 128), jnp.int32)
    live = jnp.zeros((8, 128), jnp.int32)
    for s in range(slots):
        names = jnp.where(lane_slot == s, pattern[0, s], names)
        live = jnp.where(lane_slot == s, (s < count[0]).astype(jnp.int32), live)
    place = lax.rem(z + along_z - names // ALONG_X, along_z)
    for dx in range(ALONG_X):
        there = lax.rem(x + dx, ALONG_X)
        wanted = jnp.where((lax.rem(names, ALONG_X) == there) & (live == 1), place, along_z)
        lookup_out[dx] = wanted
        if dx == 0:
            lookup_in[0] = wanted

    for f in range(bins_dev):
        at = pl.ds(f * snaps, snaps)
        measured[at, :] = measured_ref[f]
        for t in range(2):
            current[t, at, :] = map_ref[f, :, pl.ds(t * tile, tile)]
    row_bin = lax.broadcasted_iota(jnp.int32, (rows, tile), 0) // snaps
    step_size = step_ref[0]
    zeros = jnp.zeros((rows, half), jnp.bfloat16)
    lane = lax.broadcasted_iota(jnp.int32, (rows, 128), 1)

    def split(k, s, value):
        at = pl.ds((k * slots + s) * rows, rows)
        large = value.astype(jnp.bfloat16)
        pieces[at, pl.ds(0, half)] = large
        pieces[at, pl.ds(half, half)] = (value - large.astype(jnp.float32)).astype(jnp.bfloat16)


    for it in range(ITERS):
        for t in range(2):
            value = current[t]
            for f in range(bins_dev):
                sources[t, f] = jnp.where(row_bin == f, value, 0.0).astype(jnp.bfloat16)
        own, out = part_in.at[it], part_out.at[it]
        outer = [[k, k + 1] for k in range(CORES, group, CORES)]
        outer = sorted(outer, key=lambda part: group_order.index(part[1])) + [[1]]
        arrivals = []
        for batch in range(BATCHES):
            powers = jnp.zeros((rows, 128), jnp.float32)
            for i in range(few):
                s = batch * few + i
                if it == 0:
                    loads[s].wait()
                which = lax.rem(pattern[1, s], 2)
                total = jnp.zeros((rows, tile), jnp.float32)
                for f in range(bins_dev if it == 0 else 0):
                    total += lax.dot_general(
                        sources[which, f], tiles[s, f], (((1,), (1,)), ((), ())), preferred_element_type=jnp.float32
                    )
                if it > 0:
                    wide = jnp.concatenate([sources[which, f] for f in range(bins_dev)], axis=1)
                    total = jnp.dot(wide, turned[s], preferred_element_type=jnp.float32)
                largest = jnp.max(jnp.abs(total), axis=1, keepdims=True)
                power = jnp.clip(jnp.ceil(jnp.log2(jnp.maximum(largest, 1e-30))), -100.0, 128.0)
                powers = jnp.where(lane == i, power, powers)
                low, high = total[:, :half], total[:, half:]
                mine, other = jnp.where(core == 0, low, high), jnp.where(core == 0, high, low)
                split(0, s, mine)
                for dc, value in enumerate((mine, other)):
                    out[batch, dc, i] = jnp.round(value * jnp.exp2(LEVELS - power)).astype(jnp.int32).astype(jnp.int16)
            for dc in range(CORES):
                out[batch, dc, few] = powers.astype(jnp.int32).astype(jnp.int16)
            if it == 0 and batch < BATCHES - 1:
                continue
            if it == 0:
                pl.semaphore_wait(barrier, len(peers))
                (told,) = exchange([group_order], lambda k: lookup_out.at[k // CORES], lookup_in, member_at)
            for sent in (range(BATCHES) if it == 0 else [batch]):
                arrivals.append(exchange(outer, lambda k: out.at[sent, k % CORES], own.at[sent], member_at))
        if it == 0:
            told.wait_recv()
            to_smem = pltpu.make_async_copy(lookup_in, lookup_smem, smem_sem.at[0])
            to_smem.start()
            matrix_row = lax.broadcasted_iota(jnp.int32, (along_z * rows, 128), 0)
            matrix_lane = lax.broadcasted_iota(jnp.int32, (along_z * rows, 128), 1)
            matches = lax.rem(along_z - matrix_row // rows, along_z)
            same = lax.rem(matrix_row, rows) == lax.rem(matrix_lane, rows)
            for k in range(group):
                hit = same & (matches == lookup_in[k, pl.ds(0, 1), :])
                sums_matrix[:, pl.ds(k * 128, 128)] = hit.astype(jnp.float32).astype(jnp.bfloat16)
        chunks = jnp.zeros((along_z * rows, tile), jnp.float32)
        for batch in range(BATCHES):
            for part, arrival in reversed(list(zip(outer, arrivals[batch]))):
                arrival.wait_recv()
                for k in part:
                    scale = jnp.exp2(own[batch, k, few].astype(jnp.int32).astype(jnp.float32) - LEVELS)
                    for i in range(few):
                        value = own[batch, k, i].astype(jnp.int32).astype(jnp.float32)
                        split(k, batch * few + i, value * scale[:, i:i + 1])
                if batch == BATCHES - 1:
                    first, width = min(part) // CORES * CORES * slots * rows, CORES * slots * rows
                    chunks += jnp.dot(
                        sums_matrix[:, pl.ds(first, width)], pieces[pl.ds(first, width), :],
                        preferred_element_type=jnp.float32,
                    )

        def give(k):
            chunk_out[it, k] = chunks[k * rows:(k + 1) * rows, :half] + chunks[k * rows:(k + 1) * rows, half:]
            return chunk_out.at[it, k]

        (summed,) = exchange([z_order], give, chunk_in.at[it], along_at)
        total = chunks[:rows, :half] + chunks[:rows, half:] - measured[...]
        if it == 0:
            for s in range(slots):
                for f in range(bins_dev):
                    turned[s, pl.ds(f * tile, tile), :] = tiles[s, f].T
        summed.wait_recv()
        for k in range(1, along_z):
            total += chunk_in[it, k]
        held = rounded_in.at[it]
        held[0] = total.astype(jnp.bfloat16)
        held[along_z] = zeros
        (spread,) = exchange([z_order], lambda k: held.at[0], held, along_at)
        spread.wait_recv()
        if it == 0:
            to_smem.wait()
        arrivals = []
        for batch in range(BATCHES):

            def gather(k):
                asker = (ALONG_X - k // CORES) % ALONG_X * CORES + k % CORES
                there = (gather_out if k else gather_in).at[it, batch, k]
                for i in range(few):
                    there[i] = held[lookup_smem[asker, 0, (batch * few + i) * rows]]
                return there

            arrivals += exchange([group_order], gather, gather_in.at[it, batch], member_at)
            gather(0)
        gradient = [jnp.zeros((rows, tile), jnp.float32) for t in range(2)]
        for s in range(slots):
            batch, i = s // few, s % few
            if i == 0:
                arrivals[batch].wait_recv()
            which = lax.rem(pattern[1, s], 2)
            mine = gather_in[it, batch, 0, i]
            other = gather_in[it, batch, 1, i]
            for dx in range(1, ALONG_X):
                mine += gather_in[it, batch, dx * CORES, i]
                other += gather_in[it, batch, dx * CORES + 1, i]
            low = jnp.where(core == 0, mine, other).astype(jnp.float32)
            high = jnp.where(core == 0, other, mine).astype(jnp.float32)
            both = jnp.concatenate([low, high], axis=1)
            wide = jnp.concatenate([jnp.where(row_bin == f, both, 0.0) for f in range(bins_dev)], axis=1)
            product = jnp.dot(
                wide.astype(jnp.bfloat16), tiles[s].reshape(bins_dev * tile, tile), preferred_element_type=jnp.float32
            )
            for t in range(2):
                gradient[t] += jnp.where(which == t, product, 0.0)
        for t in range(2):
            moved = current[t] - step_size * gradient[t]
            current[t] = moved
            energy_in[it, 0, :, pl.ds(t * tile, tile)] = jnp.sum(moved * moved, axis=0, keepdims=True)
        energy_out[it] = energy_in[it, 0]
        (energies,) = exchange([plane_order], lambda k: energy_out.at[it], energy_in.at[it], plane_at)
        energies.wait_recv()
        energy = energy_in[it, 0]
        for k in range(1, bins):
            energy += energy_in[it, k]
        factor = jnp.maximum(0.0, 1.0 - step_size * penalty_ref[...] / jnp.sqrt(energy + 1e-06))
        for t in range(2):
            current[t] = current[t] * factor[:, t * tile:(t + 1) * tile]
    for f in range(bins_dev):
        for t in range(2):
            out_ref[f, :, pl.ds(t * tile, tile)] = current[t, pl.ds(f * snaps, snaps), :]
    for done in finish:
        done.wait_send()


def solution(mesh):
    scan, bins = mesh.shape["scan"], mesh.shape["bin"]
    along_z = scan // (ALONG_X * CORES)

    def body(tile_blocks, tile_pattern, tile_count, initial_map, measured, step_size, penalty):
        slots, bins_dev, tile, _ = tile_blocks.shape
        rows, half, group = bins_dev * initial_map.shape[1], tile // 2, ALONG_X * CORES
        points, few = initial_map.shape[2], slots // BATCHES
        bf16, f32 = jnp.bfloat16, jnp.float32
        exchanges = 1 + ((ALONG_X + 1) * BATCHES + 3) * ITERS
        hbm, smem = pl.BlockSpec(memory_space=pltpu.HBM), pl.BlockSpec(memory_space=pltpu.SMEM)
        return pl.pallas_call(
            functools.partial(kernel, along_z, bins),
            out_shape=jax.ShapeDtypeStruct(initial_map.shape, f32),
            in_specs=[hbm, hbm, smem, hbm, hbm, smem, hbm],
            out_specs=pl.BlockSpec(memory_space=pltpu.VMEM),
            scratch_shapes=[
                pltpu.SMEM(tile_pattern.shape, jnp.int32),
                pltpu.VMEM(initial_map.shape, f32),
                pltpu.VMEM(measured.shape, f32),
                pltpu.VMEM((1, points), f32),
                pltpu.VMEM((slots, bins_dev, tile, tile), bf16),
                pltpu.VMEM((slots, bins_dev * tile, tile), bf16),
                pltpu.VMEM((2, rows, tile), f32),
                pltpu.VMEM((2, bins_dev, rows, tile), bf16),
                pltpu.VMEM((rows, half), f32),
                pltpu.VMEM((ALONG_X, 8, 128), jnp.int32),
                pltpu.VMEM((group, 8, 128), jnp.int32),
                pltpu.SMEM((group, 8, 128), jnp.int32),
                pltpu.VMEM((along_z * rows, group * slots * rows), bf16),
                pltpu.VMEM((ITERS, BATCHES, CORES, few + 1, rows, half), jnp.int16),
                pltpu.VMEM((ITERS, BATCHES, group, few + 1, rows, half), jnp.int16),
                pltpu.VMEM((group * slots * rows, tile), bf16),
                pltpu.VMEM((ITERS, along_z, rows, half), f32),
                pltpu.VMEM((ITERS, along_z, rows, half), f32),
                pltpu.VMEM((ITERS, along_z + 1, rows, half), bf16),
                pltpu.VMEM((ITERS, BATCHES, group, few, rows, half), bf16),
                pltpu.VMEM((ITERS, BATCHES, group, few, rows, half), bf16),
                pltpu.VMEM((ITERS, 1, points), f32),
                pltpu.VMEM((ITERS, bins, 1, points), f32),
                pltpu.SemaphoreType.DMA((slots,)),
                pltpu.SemaphoreType.DMA((4,)),
                pltpu.SemaphoreType.DMA((1,)),
                pltpu.SemaphoreType.DMA((exchanges,)),
                pltpu.SemaphoreType.DMA((exchanges,)),
            ],
            compiler_params=pltpu.CompilerParams(
                collective_id=0, has_side_effects=True, vmem_limit_bytes=56 * 1024 * 1024
            ),
        )(tile_blocks, tile_pattern, tile_count, initial_map, measured, step_size, penalty.reshape(1, points))

    in_specs = (
        P("scan", "bin", None, None),
        P(None, "scan"),
        P("scan"),
        P("bin", None, "scan"),
        P("bin", None, "scan"),
        P(),
        P("scan"),
    )
    return jax.shard_map(body, mesh=mesh, in_specs=in_specs, out_specs=P("bin", None, "scan"), check_vma=False)
```

```python
import functools

import jax
import jax.numpy as jnp
from jax import lax
from jax.experimental import pallas as pl
from jax.experimental.pallas import tpu as pltpu
from jax.sharding import PartitionSpec as P

ITERS = 2
CORES = 2
ALONG_X = 4
MESH = pl.DeviceIdType.MESH
LEVELS = 14.9
BATCHES = 1


def kernel(along_z, bins, tiles_hbm, pattern_hbm, count_hbm, map_hbm, measured_hbm, step_hbm, penalty_hbm, out_ref,
           pattern, count, map_ref, measured_ref, step_ref, penalty_ref, tiles, turned, current, sources, measured, lookup_out, lookup_in, lookup_smem, sums_matrix,
           part_out, part_in, pieces, chunk_out, chunk_in, rounded_in, gather_out, gather_in, energy_out, energy_in,
           tile_sem, input_sem, smem_sem, send_sem, recv_sem):
    slots, bins_dev, tile, _ = tiles.shape
    group = ALONG_X * CORES
    half = tile // 2
    rows = 16
    snaps = rows // bins_dev
    few = slots // BATCHES
    scan = lax.axis_index("scan")
    y = lax.axis_index("bin")
    core = lax.rem(scan, CORES)
    x = lax.rem(scan // CORES, ALONG_X)
    z = scan // group

    def member(k):
        dx, dc = k // CORES, k % CORES
        there = (z * ALONG_X + lax.rem(x + dx, ALONG_X)) * CORES + (core if dc == 0 else 1 - core)
        return (there, y)

    def along(k):
        return (lax.rem(z + k, along_z) * group + lax.rem(scan, group), y)

    def plane(k):
        return (scan, lax.rem(y + k, bins))

    z_order = sorted(range(1, along_z), key=lambda k: -min(k, along_z - k))
    group_order = sorted(range(1, group), key=lambda k: (-min(k // CORES, ALONG_X - k // CORES), -(k % CORES)))
    plane_order = sorted(range(1, bins), key=lambda k: -min(k, bins - k))
    along_at = {k: along(k) for k in z_order}
    member_at = {k: member(k) for k in group_order}
    plane_at = {k: plane(k) for k in plane_order}
    peers = list(along_at.values()) + list(member_at.values()) + list(plane_at.values())
    barrier = pltpu.get_barrier_semaphore()
    for peer in peers:
        pl.semaphore_signal(barrier, inc=1, device_id=peer, device_id_type=MESH)
    inputs = []
    for i, (there, here) in enumerate((
        (map_hbm, map_ref), (pattern_hbm, pattern), (count_hbm, count), (measured_hbm, measured_ref), (step_hbm, step_ref),
        (penalty_hbm, penalty_ref),
    )):
        load = pltpu.make_async_copy(there, here, input_sem.at[i])
        load.start()
        inputs.append(load)
    loads = []
    for s in range(slots):
        load = pltpu.make_async_copy(tiles_hbm.at[s], tiles.at[s], tile_sem.at[s])
        load.start()
        loads.append(load)

    for load in inputs:
        load.wait()
    finish = []

    sems = iter(range(send_sem.shape[0]))

    def exchange(parts, src_of, dst, devices):
        arrivals = []
        for part in parts:
            sem = next(sems)
            for k in part:
                pltpu.make_async_remote_copy(
                    src_ref=src_of(k), dst_ref=dst.at[k], send_sem=send_sem.at[sem], recv_sem=recv_sem.at[sem],
                    device_id=devices[k], device_id_type=MESH,
                ).start()
            whole = dst.at[pl.ds(min(part), len(part))]
            arrivals.append(pltpu.make_async_remote_copy(
                src_ref=whole, dst_ref=whole, send_sem=send_sem.at[sem], recv_sem=recv_sem.at[sem],
                device_id=devices[part[0]], device_id_type=MESH,
            ))
        finish.extend(arrivals)
        return arrivals

    lane_slot = lax.broadcasted_iota(jnp.int32, (8, 128), 1) // rows
    names = jnp.zeros((8, 128), jnp.int32)
    for s in range(slots):
        names = jnp.where(lane_slot == s, pattern[0, s], names)
    place = lax.rem(z + along_z - names // ALONG_X, along_z)
    for dx in range(ALONG_X):
        there = lax.rem(x + dx, ALONG_X)
        wanted = jnp.where((lax.rem(names, ALONG_X) == there) & (lane_slot < count[...]), place, along_z)
        lookup_out[dx] = wanted
        if dx == 0:
            lookup_in[0] = wanted

    for f in range(bins_dev):
        at = pl.ds(f * snaps, snaps)
        measured[at, :] = measured_ref[f]
        for t in range(2):
            current[t, at, :] = map_ref[f, :, pl.ds(t * tile, tile)]
    row_bin = lax.broadcasted_iota(jnp.int32, (rows, tile), 0) // snaps
    step_size = step_ref[...]
    zeros = jnp.zeros((rows, half), jnp.bfloat16)
    lane = lax.broadcasted_iota(jnp.int32, (rows, 128), 1)

    def split(k, s, value):
        at = pl.ds((k * slots + s) * rows, rows)
        large = value.astype(jnp.bfloat16)
        pieces[at, pl.ds(0, half)] = large
        pieces[at, pl.ds(half, half)] = (value - large.astype(jnp.float32)).astype(jnp.bfloat16)


    for it in range(ITERS):
        for t in range(2):
            value = current[t]
            for f in range(bins_dev):
                sources[t, f] = jnp.where(row_bin == f, value, 0.0).astype(jnp.bfloat16)
        own, out = part_in.at[it], part_out.at[it]
        outer = [[k, k + 1] for k in range(CORES, group, CORES)]
        outer = sorted(outer, key=lambda part: group_order.index(part[1])) + [[1]]
        arrivals = []
        for batch in range(BATCHES):
            powers = jnp.zeros((rows, 128), jnp.float32)
            for i in range(few):
                s = batch * few + i
                if it == 0:
                    loads[s].wait()
                which = lax.rem(pattern[1, s], 2)
                total = jnp.zeros((rows, tile), jnp.float32)
                for f in range(bins_dev if it == 0 else 0):
                    total += lax.dot_general(
                        sources[which, f], tiles[s, f], (((1,), (1,)), ((), ())), preferred_element_type=jnp.float32
                    )
                if it > 0:
                    wide = jnp.concatenate([sources[which, f] for f in range(bins_dev)], axis=1)
                    total = jnp.dot(wide, turned[s], preferred_element_type=jnp.float32)
                largest = jnp.max(jnp.abs(total), axis=1, keepdims=True)
                power = jnp.clip(jnp.ceil(jnp.log2(jnp.maximum(largest, 1e-30))), -100.0, 128.0)
                powers = jnp.where(lane == i, power, powers)
                low, high = total[:, :half], total[:, half:]
                mine, other = jnp.where(core == 0, low, high), jnp.where(core == 0, high, low)
                split(0, s, mine)
                for dc, value in enumerate((mine, other)):
                    out[batch, dc, i] = jnp.round(value * jnp.exp2(LEVELS - power)).astype(jnp.int32).astype(jnp.int16)
            for dc in range(CORES):
                out[batch, dc, few] = powers.astype(jnp.int32).astype(jnp.int16)
            if it == 0 and batch < BATCHES - 1:
                continue
            if it == 0:
                pl.semaphore_wait(barrier, len(peers))
                (told,) = exchange([group_order], lambda k: lookup_out.at[k // CORES], lookup_in, member_at)
            for sent in (range(BATCHES) if it == 0 else [batch]):
                arrivals.append(exchange(outer, lambda k: out.at[sent, k % CORES], own.at[sent], member_at))
        if it == 0:
            told.wait_recv()
            to_smem = pltpu.make_async_copy(lookup_in, lookup_smem, smem_sem.at[0])
            to_smem.start()
            matrix_row = lax.broadcasted_iota(jnp.int32, (along_z * rows, 128), 0)
            matrix_lane = lax.broadcasted_iota(jnp.int32, (along_z * rows, 128), 1)
            matches = lax.rem(along_z - matrix_row // rows, along_z)
            same = lax.rem(matrix_row, rows) == lax.rem(matrix_lane, rows)
            for k in range(group):
                hit = same & (matches == lookup_in[k, pl.ds(0, 1), :])
                sums_matrix[:, pl.ds(k * 128, 128)] = hit.astype(jnp.float32).astype(jnp.bfloat16)
        chunks = jnp.zeros((along_z * rows, tile), jnp.float32)
        for batch in range(BATCHES):
            for part, arrival in reversed(list(zip(outer, arrivals[batch]))):
                arrival.wait_recv()
                for k in part:
                    scale = jnp.exp2(own[batch, k, few].astype(jnp.int32).astype(jnp.float32) - LEVELS)
                    for i in range(few):
                        value = own[batch, k, i].astype(jnp.int32).astype(jnp.float32)
                        split(k, batch * few + i, value * scale[:, i:i + 1])
                if batch == BATCHES - 1:
                    first, width = min(part) // CORES * CORES * slots * rows, CORES * slots * rows
                    chunks += jnp.dot(
                        sums_matrix[:, pl.ds(first, width)], pieces[pl.ds(first, width), :],
                        preferred_element_type=jnp.float32,
                    )

        def give(k):
            chunk_out[it, k] = chunks[k * rows:(k + 1) * rows, :half] + chunks[k * rows:(k + 1) * rows, half:]
            return chunk_out.at[it, k]

        (summed,) = exchange([z_order], give, chunk_in.at[it], along_at)
        total = chunks[:rows, :half] + chunks[:rows, half:] - measured[...]
        if it == 0:
            for s in range(slots):
                for f in range(bins_dev):
                    turned[s, pl.ds(f * tile, tile), :] = tiles[s, f].T
        summed.wait_recv()
        for k in range(1, along_z):
            total += chunk_in[it, k]
        held = rounded_in.at[it]
        held[0] = total.astype(jnp.bfloat16)
        held[along_z] = zeros
        (spread,) = exchange([z_order], lambda k: held.at[0], held, along_at)
        spread.wait_recv()
        if it == 0:
            to_smem.wait()
        arrivals = []
        for batch in range(BATCHES):

            def gather(k):
                asker = (ALONG_X - k // CORES) % ALONG_X * CORES + k % CORES
                there = (gather_out if k else gather_in).at[it, batch, k]
                for i in range(few):
                    there[i] = held[lookup_smem[asker, 0, (batch * few + i) * rows]]
                return there

            arrivals += exchange([group_order], gather, gather_in.at[it, batch], member_at)
            gather(0)
        gradient = [jnp.zeros((rows, tile), jnp.float32) for t in range(2)]
        for s in range(slots):
            batch, i = s // few, s % few
            if i == 0:
                arrivals[batch].wait_recv()
            which = lax.rem(pattern[1, s], 2)
            mine = gather_in[it, batch, 0, i]
            other = gather_in[it, batch, 1, i]
            for dx in range(1, ALONG_X):
                mine += gather_in[it, batch, dx * CORES, i]
                other += gather_in[it, batch, dx * CORES + 1, i]
            low = jnp.where(core == 0, mine, other).astype(jnp.float32)
            high = jnp.where(core == 0, other, mine).astype(jnp.float32)
            both = jnp.concatenate([low, high], axis=1)
            wide = jnp.concatenate([jnp.where(row_bin == f, both, 0.0) for f in range(bins_dev)], axis=1)
            product = jnp.dot(
                wide.astype(jnp.bfloat16), tiles[s].reshape(bins_dev * tile, tile), preferred_element_type=jnp.float32
            )
            for t in range(2):
                gradient[t] += jnp.where(which == t, product, 0.0)
        for t in range(2):
            moved = current[t] - step_size * gradient[t]
            current[t] = moved
            energy_in[it, 0, :, pl.ds(t * tile, tile)] = jnp.sum(moved * moved, axis=0, keepdims=True)
        energy_out[it] = energy_in[it, 0]
        (energies,) = exchange([plane_order], lambda k: energy_out.at[it], energy_in.at[it], plane_at)
        energies.wait_recv()
        energy = energy_in[it, 0]
        for k in range(1, bins):
            energy += energy_in[it, k]
        factor = jnp.maximum(0.0, 1.0 - step_size * penalty_ref[...] / jnp.sqrt(energy + 1e-06))
        for t in range(2):
            current[t] = current[t] * factor[:, t * tile:(t + 1) * tile]
    for f in range(bins_dev):
        for t in range(2):
            out_ref[f, :, pl.ds(t * tile, tile)] = current[t, pl.ds(f * snaps, snaps), :]
    for done in finish:
        done.wait_send()


def solution(mesh):
    scan, bins = mesh.shape["scan"], mesh.shape["bin"]
    along_z = scan // (ALONG_X * CORES)

    def body(tile_blocks, tile_pattern, tile_count, initial_map, measured, step_size, penalty):
        slots, bins_dev, tile, _ = tile_blocks.shape
        rows, half, group = bins_dev * initial_map.shape[1], tile // 2, ALONG_X * CORES
        points, few = initial_map.shape[2], slots // BATCHES
        bf16, f32 = jnp.bfloat16, jnp.float32
        exchanges = 1 + ((ALONG_X + 1) * BATCHES + 3) * ITERS
        hbm = pl.BlockSpec(memory_space=pltpu.HBM)
        return pl.pallas_call(
            functools.partial(kernel, along_z, bins),
            out_shape=jax.ShapeDtypeStruct(initial_map.shape, f32),
            in_specs=[hbm] * 7,
            out_specs=pl.BlockSpec(memory_space=pltpu.VMEM),
            scratch_shapes=[
                pltpu.SMEM(tile_pattern.shape, jnp.int32),
                pltpu.VMEM((1, 1), jnp.int32),
                pltpu.VMEM(initial_map.shape, f32),
                pltpu.VMEM(measured.shape, f32),
                pltpu.VMEM((1, 1), f32),
                pltpu.VMEM((1, points), f32),
                pltpu.VMEM((slots, bins_dev, tile, tile), bf16),
                pltpu.VMEM((slots, bins_dev * tile, tile), bf16),
                pltpu.VMEM((2, rows, tile), f32),
                pltpu.VMEM((2, bins_dev, rows, tile), bf16),
                pltpu.VMEM((rows, half), f32),
                pltpu.VMEM((ALONG_X, 8, 128), jnp.int32),
                pltpu.VMEM((group, 8, 128), jnp.int32),
                pltpu.SMEM((group, 8, 128), jnp.int32),
                pltpu.VMEM((along_z * rows, group * slots * rows), bf16),
                pltpu.VMEM((ITERS, BATCHES, CORES, few + 1, rows, half), jnp.int16),
                pltpu.VMEM((ITERS, BATCHES, group, few + 1, rows, half), jnp.int16),
                pltpu.VMEM((group * slots * rows, tile), bf16),
                pltpu.VMEM((ITERS, along_z, rows, half), f32),
                pltpu.VMEM((ITERS, along_z, rows, half), f32),
                pltpu.VMEM((ITERS, along_z + 1, rows, half), bf16),
                pltpu.VMEM((ITERS, BATCHES, group, few, rows, half), bf16),
                pltpu.VMEM((ITERS, BATCHES, group, few, rows, half), bf16),
                pltpu.VMEM((ITERS, 1, points), f32),
                pltpu.VMEM((ITERS, bins, 1, points), f32),
                pltpu.SemaphoreType.DMA((slots,)),
                pltpu.SemaphoreType.DMA((6,)),
                pltpu.SemaphoreType.DMA((1,)),
                pltpu.SemaphoreType.DMA((exchanges,)),
                pltpu.SemaphoreType.DMA((exchanges,)),
            ],
            compiler_params=pltpu.CompilerParams(
                collective_id=0, has_side_effects=True, vmem_limit_bytes=56 * 1024 * 1024
            ),
        )(
            tile_blocks, tile_pattern, tile_count.reshape(1, 1), initial_map, measured, step_size.reshape(1, 1),
            penalty.reshape(1, points),
        )

    in_specs = (
        P("scan", "bin", None, None),
        P(None, "scan"),
        P("scan"),
        P("bin", None, "scan"),
        P("bin", None, "scan"),
        P(),
        P("scan"),
    )
    return jax.shard_map(body, mesh=mesh, in_specs=in_specs, out_specs=P("bin", None, "scan"), check_vma=False)
```

```python
import functools

import jax
import jax.numpy as jnp
from jax import lax
from jax.experimental import pallas as pl
from jax.experimental.pallas import tpu as pltpu
from jax.sharding import PartitionSpec as P

ITERS = 2
CORES = 2
ALONG_X = 4
MESH = pl.DeviceIdType.MESH
LEVELS = 14.9
BATCHES = 1


def kernel(along_z, bins, tiles_hbm, pattern, count_hbm, map_hbm, measured_hbm, step_hbm, penalty_hbm, out_ref,
           count, map_ref, measured_ref, step_ref, penalty_ref, tiles, turned, current, sources, measured, lookup_out, lookup_in, lookup_smem, sums_matrix,
           part_out, part_in, pieces, chunk_out, chunk_in, rounded_in, gather_out, gather_in, energy_out, energy_in,
           tile_sem, input_sem, smem_sem, send_sem, recv_sem):
    slots, bins_dev, tile, _ = tiles.shape
    group = ALONG_X * CORES
    half = tile // 2
    rows = 16
    snaps = rows // bins_dev
    few = slots // BATCHES
    scan = lax.axis_index("scan")
    y = lax.axis_index("bin")
    core = lax.rem(scan, CORES)
    x = lax.rem(scan // CORES, ALONG_X)
    z = scan // group

    def member(k):
        dx, dc = k // CORES, k % CORES
        there = (z * ALONG_X + lax.rem(x + dx, ALONG_X)) * CORES + (core if dc == 0 else 1 - core)
        return (there, y)

    def along(k):
        return (lax.rem(z + k, along_z) * group + lax.rem(scan, group), y)

    def plane(k):
        return (scan, lax.rem(y + k, bins))

    z_order = sorted(range(1, along_z), key=lambda k: -min(k, along_z - k))
    group_order = sorted(range(1, group), key=lambda k: (-min(k // CORES, ALONG_X - k // CORES), -(k % CORES)))
    plane_order = sorted(range(1, bins), key=lambda k: -min(k, bins - k))
    along_at = {k: along(k) for k in z_order}
    member_at = {k: member(k) for k in group_order}
    plane_at = {k: plane(k) for k in plane_order}
    peers = list(along_at.values()) + list(member_at.values()) + list(plane_at.values())
    barrier = pltpu.get_barrier_semaphore()
    for peer in peers:
        pl.semaphore_signal(barrier, inc=1, device_id=peer, device_id_type=MESH)
    inputs = []
    for i, (there, here) in enumerate((
        (map_hbm, map_ref), (count_hbm, count), (measured_hbm, measured_ref), (step_hbm, step_ref),
        (penalty_hbm, penalty_ref),
    )):
        load = pltpu.make_async_copy(there, here, input_sem.at[i])
        load.start()
        inputs.append(load)
    loads = []
    for s in range(slots):
        load = pltpu.make_async_copy(tiles_hbm.at[s], tiles.at[s], tile_sem.at[s])
        load.start()
        loads.append(load)

    for load in inputs:
        load.wait()
    finish = []

    sems = iter(range(send_sem.shape[0]))

    def exchange(parts, src_of, dst, devices):
        arrivals = []
        for part in parts:
            sem = next(sems)
            for k in part:
                pltpu.make_async_remote_copy(
                    src_ref=src_of(k), dst_ref=dst.at[k], send_sem=send_sem.at[sem], recv_sem=recv_sem.at[sem],
                    device_id=devices[k], device_id_type=MESH,
                ).start()
            whole = dst.at[pl.ds(min(part), len(part))]
            arrivals.append(pltpu.make_async_remote_copy(
                src_ref=whole, dst_ref=whole, send_sem=send_sem.at[sem], recv_sem=recv_sem.at[sem],
                device_id=devices[part[0]], device_id_type=MESH,
            ))
        finish.extend(arrivals)
        return arrivals

    lane_slot = lax.broadcasted_iota(jnp.int32, (8, 128), 1) // rows
    names = jnp.zeros((8, 128), jnp.int32)
    for s in range(slots):
        names = jnp.where(lane_slot == s, pattern[0, s], names)
    place = lax.rem(z + along_z - names // ALONG_X, along_z)
    for dx in range(ALONG_X):
        there = lax.rem(x + dx, ALONG_X)
        wanted = jnp.where((lax.rem(names, ALONG_X) == there) & (lane_slot < count[...]), place, along_z)
        lookup_out[dx] = wanted
        if dx == 0:
            lookup_in[0] = wanted

    for f in range(bins_dev):
        at = pl.ds(f * snaps, snaps)
        measured[at, :] = measured_ref[f]
        for t in range(2):
            current[t, at, :] = map_ref[f, :, pl.ds(t * tile, tile)]
    row_bin = lax.broadcasted_iota(jnp.int32, (rows, tile), 0) // snaps
    step_size = step_ref[...]
    zeros = jnp.zeros((rows, half), jnp.bfloat16)
    lane = lax.broadcasted_iota(jnp.int32, (rows, 128), 1)

    def split(k, s, value):
        at = pl.ds((k * slots + s) * rows, rows)
        large = value.astype(jnp.bfloat16)
        pieces[at, pl.ds(0, half)] = large
        pieces[at, pl.ds(half, half)] = (value - large.astype(jnp.float32)).astype(jnp.bfloat16)


    for it in range(ITERS):
        for t in range(2):
            value = current[t]
            for f in range(bins_dev):
                sources[t, f] = jnp.where(row_bin == f, value, 0.0).astype(jnp.bfloat16)
        own, out = part_in.at[it], part_out.at[it]
        outer = [[k, k + 1] for k in range(CORES, group, CORES)]
        outer = sorted(outer, key=lambda part: group_order.index(part[1])) + [[1]]
        arrivals = []
        for batch in range(BATCHES):
            powers = jnp.zeros((rows, 128), jnp.float32)
            for i in range(few):
                s = batch * few + i
                if it == 0:
                    loads[s].wait()
                which = lax.rem(pattern[1, s], 2)
                total = jnp.zeros((rows, tile), jnp.float32)
                for f in range(bins_dev if it == 0 else 0):
                    total += lax.dot_general(
                        sources[which, f], tiles[s, f], (((1,), (1,)), ((), ())), preferred_element_type=jnp.float32
                    )
                if it > 0:
                    wide = jnp.concatenate([sources[which, f] for f in range(bins_dev)], axis=1)
                    total = jnp.dot(wide, turned[s], preferred_element_type=jnp.float32)
                largest = jnp.max(jnp.abs(total), axis=1, keepdims=True)
                power = jnp.clip(jnp.ceil(jnp.log2(jnp.maximum(largest, 1e-30))), -100.0, 128.0)
                powers = jnp.where(lane == i, power, powers)
                low, high = total[:, :half], total[:, half:]
                mine, other = jnp.where(core == 0, low, high), jnp.where(core == 0, high, low)
                split(0, s, mine)
                for dc, value in enumerate((mine, other)):
                    out[batch, dc, i] = jnp.round(value * jnp.exp2(LEVELS - power)).astype(jnp.int32).astype(jnp.int16)
            for dc in range(CORES):
                out[batch, dc, few] = powers.astype(jnp.int32).astype(jnp.int16)
            if it == 0 and batch < BATCHES - 1:
                continue
            if it == 0:
                pl.semaphore_wait(barrier, len(peers))
                (told,) = exchange([group_order], lambda k: lookup_out.at[k // CORES], lookup_in, member_at)
            for sent in (range(BATCHES) if it == 0 else [batch]):
                arrivals.append(exchange(outer, lambda k: out.at[sent, k % CORES], own.at[sent], member_at))
        if it == 0:
            told.wait_recv()
            to_smem = pltpu.make_async_copy(lookup_in, lookup_smem, smem_sem.at[0])
            to_smem.start()
            matrix_row = lax.broadcasted_iota(jnp.int32, (along_z * rows, 128), 0)
            matrix_lane = lax.broadcasted_iota(jnp.int32, (along_z * rows, 128), 1)
            matches = lax.rem(along_z - matrix_row // rows, along_z)
            same = lax.rem(matrix_row, rows) == lax.rem(matrix_lane, rows)
            for k in range(group):
                hit = same & (matches == lookup_in[k, pl.ds(0, 1), :])
                sums_matrix[:, pl.ds(k * 128, 128)] = hit.astype(jnp.float32).astype(jnp.bfloat16)
        chunks = jnp.zeros((along_z * rows, tile), jnp.float32)
        for batch in range(BATCHES):
            for part, arrival in reversed(list(zip(outer, arrivals[batch]))):
                arrival.wait_recv()
                for k in part:
                    scale = jnp.exp2(own[batch, k, few].astype(jnp.int32).astype(jnp.float32) - LEVELS)
                    for i in range(few):
                        value = own[batch, k, i].astype(jnp.int32).astype(jnp.float32)
                        split(k, batch * few + i, value * scale[:, i:i + 1])
                if batch == BATCHES - 1:
                    first, width = min(part) // CORES * CORES * slots * rows, CORES * slots * rows
                    chunks += jnp.dot(
                        sums_matrix[:, pl.ds(first, width)], pieces[pl.ds(first, width), :],
                        preferred_element_type=jnp.float32,
                    )

        def give(k):
            chunk_out[it, k] = chunks[k * rows:(k + 1) * rows, :half] + chunks[k * rows:(k + 1) * rows, half:]
            return chunk_out.at[it, k]

        (summed,) = exchange([z_order], give, chunk_in.at[it], along_at)
        total = chunks[:rows, :half] + chunks[:rows, half:] - measured[...]
        if it == 0:
            for s in range(slots):
                for f in range(bins_dev):
                    turned[s, pl.ds(f * tile, tile), :] = tiles[s, f].T
        summed.wait_recv()
        for k in range(1, along_z):
            total += chunk_in[it, k]
        held = rounded_in.at[it]
        held[0] = total.astype(jnp.bfloat16)
        held[along_z] = zeros
        (spread,) = exchange([z_order], lambda k: held.at[0], held, along_at)
        spread.wait_recv()
        if it == 0:
            to_smem.wait()
        arrivals = []
        for batch in range(BATCHES):

            def gather(k):
                asker = (ALONG_X - k // CORES) % ALONG_X * CORES + k % CORES
                there = (gather_out if k else gather_in).at[it, batch, k]
                for i in range(few):
                    there[i] = held[lookup_smem[asker, 0, (batch * few + i) * rows]]
                return there

            arrivals += exchange([group_order], gather, gather_in.at[it, batch], member_at)
            gather(0)
        gradient = [jnp.zeros((rows, tile), jnp.float32) for t in range(2)]
        for s in range(slots):
            batch, i = s // few, s % few
            if i == 0:
                arrivals[batch].wait_recv()
            which = lax.rem(pattern[1, s], 2)
            mine = gather_in[it, batch, 0, i]
            other = gather_in[it, batch, 1, i]
            for dx in range(1, ALONG_X):
                mine += gather_in[it, batch, dx * CORES, i]
                other += gather_in[it, batch, dx * CORES + 1, i]
            low = jnp.where(core == 0, mine, other).astype(jnp.float32)
            high = jnp.where(core == 0, other, mine).astype(jnp.float32)
            both = jnp.concatenate([low, high], axis=1)
            wide = jnp.concatenate([jnp.where(row_bin == f, both, 0.0) for f in range(bins_dev)], axis=1)
            product = jnp.dot(
                wide.astype(jnp.bfloat16), tiles[s].reshape(bins_dev * tile, tile), preferred_element_type=jnp.float32
            )
            for t in range(2):
                gradient[t] += jnp.where(which == t, product, 0.0)
        for t in range(2):
            moved = current[t] - step_size * gradient[t]
            current[t] = moved
            energy_in[it, 0, :, pl.ds(t * tile, tile)] = jnp.sum(moved * moved, axis=0, keepdims=True)
        energy_out[it] = energy_in[it, 0]
        (energies,) = exchange([plane_order], lambda k: energy_out.at[it], energy_in.at[it], plane_at)
        energies.wait_recv()
        energy = energy_in[it, 0]
        for k in range(1, bins):
            energy += energy_in[it, k]
        factor = jnp.maximum(0.0, 1.0 - step_size * penalty_ref[...] / jnp.sqrt(energy + 1e-06))
        for t in range(2):
            current[t] = current[t] * factor[:, t * tile:(t + 1) * tile]
    for f in range(bins_dev):
        for t in range(2):
            out_ref[f, :, pl.ds(t * tile, tile)] = current[t, pl.ds(f * snaps, snaps), :]
    for done in finish:
        done.wait_send()


def solution(mesh):
    scan, bins = mesh.shape["scan"], mesh.shape["bin"]
    along_z = scan // (ALONG_X * CORES)

    def body(tile_blocks, tile_pattern, tile_count, initial_map, measured, step_size, penalty):
        slots, bins_dev, tile, _ = tile_blocks.shape
        rows, half, group = bins_dev * initial_map.shape[1], tile // 2, ALONG_X * CORES
        points, few = initial_map.shape[2], slots // BATCHES
        bf16, f32 = jnp.bfloat16, jnp.float32
        exchanges = 1 + ((ALONG_X + 1) * BATCHES + 3) * ITERS
        hbm = pl.BlockSpec(memory_space=pltpu.HBM)
        return pl.pallas_call(
            functools.partial(kernel, along_z, bins),
            out_shape=jax.ShapeDtypeStruct(initial_map.shape, f32),
            in_specs=[hbm, pl.BlockSpec(memory_space=pltpu.SMEM)] + [hbm] * 5,
            out_specs=pl.BlockSpec(memory_space=pltpu.VMEM),
            scratch_shapes=[
                pltpu.VMEM((1, 1), jnp.int32),
                pltpu.VMEM(initial_map.shape, f32),
                pltpu.VMEM(measured.shape, f32),
                pltpu.VMEM((1, 1), f32),
                pltpu.VMEM((1, points), f32),
                pltpu.VMEM((slots, bins_dev, tile, tile), bf16),
                pltpu.VMEM((slots, bins_dev * tile, tile), bf16),
                pltpu.VMEM((2, rows, tile), f32),
                pltpu.VMEM((2, bins_dev, rows, tile), bf16),
                pltpu.VMEM((rows, half), f32),
                pltpu.VMEM((ALONG_X, 8, 128), jnp.int32),
                pltpu.VMEM((group, 8, 128), jnp.int32),
                pltpu.SMEM((group, 8, 128), jnp.int32),
                pltpu.VMEM((along_z * rows, group * slots * rows), bf16),
                pltpu.VMEM((ITERS, BATCHES, CORES, few + 1, rows, half), jnp.int16),
                pltpu.VMEM((ITERS, BATCHES, group, few + 1, rows, half), jnp.int16),
                pltpu.VMEM((group * slots * rows, tile), bf16),
                pltpu.VMEM((ITERS, along_z, rows, half), f32),
                pltpu.VMEM((ITERS, along_z, rows, half), f32),
                pltpu.VMEM((ITERS, along_z + 1, rows, half), bf16),
                pltpu.VMEM((ITERS, BATCHES, group, few, rows, half), bf16),
                pltpu.VMEM((ITERS, BATCHES, group, few, rows, half), bf16),
                pltpu.VMEM((ITERS, 1, points), f32),
                pltpu.VMEM((ITERS, bins, 1, points), f32),
                pltpu.SemaphoreType.DMA((slots,)),
                pltpu.SemaphoreType.DMA((5,)),
                pltpu.SemaphoreType.DMA((1,)),
                pltpu.SemaphoreType.DMA((exchanges,)),
                pltpu.SemaphoreType.DMA((exchanges,)),
            ],
            compiler_params=pltpu.CompilerParams(
                collective_id=0, has_side_effects=True, vmem_limit_bytes=55168 * 1024
            ),
        )(
            tile_blocks, tile_pattern, tile_count.reshape(1, 1), initial_map, measured, step_size.reshape(1, 1),
            penalty.reshape(1, points),
        )

    in_specs = (
        P("scan", "bin", None, None),
        P(None, "scan"),
        P("scan"),
        P("bin", None, "scan"),
        P("bin", None, "scan"),
        P(),
        P("scan"),
    )
    return jax.shard_map(body, mesh=mesh, in_specs=in_specs, out_specs=P("bin", None, "scan"), check_vma=False)
```
